32 devices in a mesh: dom: 8 (over y, x, core), feat: 4 (over z).
Axes of the slice: x: 2, y: 2, z: 4, core: 2. Of those that a mesh axis runs over, the one named last changes fastest.
Arguments:
- features: bfloat16 [24576, 1024], P('dom', 'feat'), may hold values from -6 to 6
- w_self: bfloat16 [1024, 256], P('feat'), may hold values from -0.1875 to 0.1875
- w_neigh: bfloat16 [1024, 256], P('feat'), may hold values from -0.1875 to 0.1875
- tile_weights: bfloat16 [192, 20, 128, 128], P(('dom', 'feat')), may hold values from 0.004 to 10.5, as said below
- local_refs: int32 [192, 4], P(('dom', 'feat')), may hold values from 0 to 5
- remote_refs: int32 [192, 16], P(('dom', 'feat')), may hold values from 0 to 95, as said below
- send_tiles: int32 [32, 8, 12], P(('dom', 'feat')), may hold values from 0 to 5
- out_grad: bfloat16 [24576, 256], P(('dom', 'feat')), may hold values from -6 to 6
Outputs:
- hidden: bfloat16 [24576, 256], P(('dom', 'feat'))
- grad_features: bfloat16 [24576, 1024], P('dom', 'feat')
- grad_self: float32 [1024, 256], P('feat')
- grad_neigh: float32 [1024, 256], P('feat')
The draws below stay inside these ranges and needn't reach their ends.
Inputs may be any that keep to these rules, and one draw needn't show every extreme that they name: For each node block, the 96 entries of remote_refs on its tiles name every received slot exactly once. `tile_weights`: positive edge weights.
All inputs are finite; a program needn't handle non-finite values.
Results may differ from the reference program's by a relative error of at most 0.0062.
Values may be sent and summed in bfloat16 or wider, within the bound.
A program may use at most 128 MiB of HBM per device.

```python
import math
import jax
import jax.numpy as jnp
from jax import lax

F = 1024
H = 256
TILE = 128
KL = 4
KR = 16
NT = 6
K = 20
SLOTS = 12
NODES = 24576
NTILES = 192
N_DOM = 8
N_FEAT = 4


def draw_tile_weights(key, part):
    key = jax.random.fold_in(key, 7)
    key_rows, key_cols, key_base = jax.random.split(key, 3)
    shape = (NTILES, K, TILE, TILE)
    row_scale = jnp.exp(jax.random.uniform(key_rows, (NTILES, 1, TILE, 1), jnp.float32, math.log(0.1), 0.0))
    col_scale = jnp.exp(jax.random.uniform(key_cols, (NTILES, K, 1, TILE), jnp.float32, 0.0, math.log(10.0)))
    base = jax.random.uniform(key_base, shape, jnp.float32, 0.2, 1.0)
    return (row_scale * col_scale * base).astype(jnp.bfloat16)


def draw_remote_refs(key, part):
    key = jax.random.fold_in(key, 11)
    keys = jax.random.split(key, N_DOM * N_FEAT)
    orders = jax.vmap(lambda single: jax.random.permutation(single, NT * KR))(keys)
    return orders.reshape(NTILES, KR).astype(jnp.int32)


def place_ends(entries, rng, smallest, largest):
    spot = [jax.random.randint(jax.random.fold_in(rng, axis), (), 0, length) for axis, length in enumerate(entries.shape)]
    longest = entries.shape.index(max(entries.shape))
    neighbour = spot[:longest] + [(spot[longest] + 1) % entries.shape[longest]] + spot[longest + 1:]
    return entries.at[tuple(spot)].set(smallest).at[tuple(neighbour)].set(largest)


def strengthened(drawn, own_key, source, target, shards_of, factor):
    owner, partner = [(jnp.arange(drawn.shape[axis_at]) // (drawn.shape[axis_at] // shards_of)).reshape([-1 if axis == axis_at else 1 for axis in range(drawn.ndim)]) for axis_at in (source, target)]
    chosen = jax.random.permutation(own_key, shards_of)[partner]
    strong = (owner == chosen) | (owner == (partner + shards_of // 2) % shards_of)
    return jnp.where(strong, factor * drawn, drawn)


def block_scale(key, shape, pieces, smallest, top_value):
    factor_of, own = 1.0, jax.random.fold_in(key, 6)
    for dim, blocks in pieces:
        draws = jnp.exp(jax.random.uniform(jax.random.fold_in(own, dim), (blocks,), jnp.float32, smallest / len(pieces), top_value / len(pieces)))
        factor_of = factor_of * jnp.repeat(draws, shape[dim] // blocks).reshape([-1 if axis == dim else 1 for axis in range(len(shape))])
    return factor_of


def bell_draw(stream_key, dims, deviation, limit, cuts=(), kind=jnp.bfloat16):
    drawn = deviation * jax.random.normal(stream_key, dims, jnp.float32)
    if cuts:
        drawn = drawn * block_scale(stream_key, dims, cuts, -0.22, 0.18)
    return jnp.clip(drawn, -limit, limit).astype(kind)


def bell_draw_with(rng, extent, spread, most, pieces, heavy, held_as=jnp.bfloat16):
    result = spread * jax.random.normal(rng, extent, jnp.float32)
    if pieces:
        result = result * block_scale(rng, extent, pieces, -0.22, 0.18)
    return jnp.clip(strengthened(result, jax.random.fold_in(rng, 3), *heavy), -most, most).astype(held_as)


def setup_inputs(seed: int = 0) -> dict:
    streams_of = jax.random.split(jax.random.key(seed), 9)
    return {
        "features": bell_draw_with(streams_of[0], (NODES, F), 1.0, 6.0, ((0, 8), (1, 4)), (1, 0, 8, 2.0)),
        "w_self": bell_draw(streams_of[1], (F, H), F ** -0.5, 0.1875, ((0, 4),)),
        "w_neigh": bell_draw(streams_of[2], (F, H), F ** -0.5, 0.1875, ((0, 4),)),
        "tile_weights": draw_tile_weights(jax.random.fold_in(streams_of[8], 71), 0),
        "local_refs": place_ends(jax.random.randint(streams_of[4], (NTILES, KL), 0, NT), jax.random.fold_in(streams_of[4], 1), 0, NT - 1).astype(jnp.int32),
        "remote_refs": draw_remote_refs(jax.random.fold_in(streams_of[8], 71), 0),
        "send_tiles": place_ends(jax.random.randint(streams_of[6], (N_DOM * N_FEAT, N_DOM, SLOTS), 0, NT), jax.random.fold_in(streams_of[6], 1), 0, NT - 1).astype(jnp.int32),
        "out_grad": bell_draw(streams_of[7], (NODES, H), 1.0, 6.0, ((0, 32),)),
    }


def reference(features, w_self, w_neigh, tile_weights, local_refs, remote_refs, send_tiles, out_grad):
    groups = N_DOM * N_FEAT
    highest = lax.Precision.HIGHEST
    w_both = jnp.concatenate([w_self, w_neigh], axis=1)
    projected = jnp.dot(features, w_both, preferred_element_type=jnp.float32)
    self_part = projected[:, :H]
    neigh_tiles = projected[:, H:].astype(jnp.bfloat16).reshape(NTILES, TILE, H)
    slot_index = jnp.arange(N_DOM * SLOTS, dtype=jnp.int32)
    source_dom = slot_index // SLOTS
    slot_number = slot_index % SLOTS
    device = jnp.arange(groups, dtype=jnp.int32)
    dom_of = device // N_FEAT
    slice_of = device % N_FEAT
    source_block = source_dom[None, :] * N_FEAT + slice_of[:, None]
    received_ids = source_block * NT + send_tiles[source_block, dom_of[:, None], slot_number[None, :]]
    owner_block = jnp.arange(NTILES, dtype=jnp.int32) // NT
    local_ids = owner_block[:, None] * NT + local_refs
    remote_ids = received_ids[owner_block[:, None], remote_refs]
    source_ids = jnp.concatenate([local_ids, remote_ids], axis=1).astype(jnp.int32).reshape(groups, NT, K)
    weights = tile_weights.reshape(groups, NT, K, TILE, TILE)

    def forward_block(packed):
        indices, block_weights = packed
        weights32 = block_weights.astype(jnp.float32)
        sources = neigh_tiles[indices].astype(jnp.float32)
        summed = jnp.einsum('tkij,tkjh->tih', weights32, sources, precision=highest)
        return (summed, lax.optimization_barrier(jnp.sum(weights32, axis=(1, 3))))
    summed, degree = lax.map(forward_block, (source_ids, weights))
    root_degree = jnp.sqrt(degree).reshape(NTILES, TILE, 1)
    aggregated = (summed.reshape(NTILES, TILE, H) / root_degree).reshape(NODES, H)
    preact = self_part + aggregated
    hidden = jax.nn.silu(preact).astype(jnp.bfloat16)
    logistic = jax.nn.sigmoid(preact)
    grad_pre = out_grad.astype(jnp.float32) * (logistic * (1.0 + preact * (1.0 - logistic)))
    grad_self_rows = grad_pre.astype(jnp.bfloat16)
    grad_agg = (grad_pre.reshape(NTILES, TILE, H) / root_degree).astype(jnp.bfloat16).reshape(groups, NT, TILE, H)

    def backward_block(running, packed):
        indices, block_weights, grads = packed
        contrib = jnp.einsum('tkij,tih->tkjh', block_weights.astype(jnp.float32), grads.astype(jnp.float32), precision=highest)
        local_terms = contrib[:, :KL]
        remote_terms = lax.optimization_barrier(contrib[:, KL:].astype(jnp.bfloat16)).astype(jnp.float32)
        running = running.at[indices[:, :KL].reshape(-1)].add(local_terms.reshape(-1, TILE, H))
        running = running.at[indices[:, KL:].reshape(-1)].add(remote_terms.reshape(-1, TILE, H))
        return (running, None)
    grad_neigh_nodes, _ = lax.scan(backward_block, jnp.zeros((NTILES, TILE, H), jnp.float32), (source_ids, weights, grad_agg))
    grad_proj = jnp.concatenate([grad_self_rows, grad_neigh_nodes.reshape(NODES, H).astype(jnp.bfloat16)], axis=1)
    grad_features = jnp.dot(grad_proj, w_both.T, preferred_element_type=jnp.float32).astype(jnp.bfloat16)
    grad_w = jnp.dot(features.T, grad_proj, preferred_element_type=jnp.float32) * float(NODES) ** (-0.5)
    return (hidden, grad_features, grad_w[:, :H], grad_w[:, H:])
```

```python
import functools
import math

import jax
import jax.numpy as jnp
from jax import lax
from jax.experimental import pallas as pl
from jax.experimental.pallas import tpu as pltpu
from jax.sharding import PartitionSpec as P

MESH = pl.DeviceIdType.MESH
F32 = jnp.float32
BF16 = jnp.bfloat16
LANES = 8
HALVES = 2
ORDERS = 2
VMEM_LIMIT = 60 * 1024 * 1024


def send(src, dst, send_sem, recv_sem, where):
    copy = pltpu.make_async_remote_copy(
        src_ref=src, dst_ref=dst, send_sem=send_sem, recv_sem=recv_sem,
        device_id=where, device_id_type=MESH,
    )
    copy.start()
    return copy


def arrived(ref, sem):
    pltpu.make_async_remote_copy(
        src_ref=ref, dst_ref=ref, send_sem=sem, recv_sem=sem,
        device_id={"feat": lax.axis_index("feat")}, device_id_type=MESH,
    ).wait_recv()


def greet(dom_count, feat_count):
    d, z = lax.axis_index("dom"), lax.axis_index("feat")
    barrier = pltpu.get_barrier_semaphore()
    for i in range(1, dom_count):
        pl.semaphore_signal(
            barrier, inc=1, device_id={"dom": lax.rem(d + i, dom_count)}, device_id_type=MESH
        )
    for i in range(1, feat_count):
        pl.semaphore_signal(
            barrier, inc=1, device_id={"feat": lax.rem(z + i, feat_count)}, device_id_type=MESH
        )
    pl.semaphore_wait(barrier, dom_count + feat_count - 2)


def rows_at(start, size, unit):
    return pl.ds(pl.multiple_of(start, unit), size)


def project_kernel(
    sizes, features, w_self, w_neigh, slots, own, w_full, self_part, gathered, table,
    local_sem, w1s, w1r, w2s, w2r, fs, fr, ts, tr, s1, s2, s3, agr,
):
    dom_count, nf, rows, fl, hidden, n = sizes
    d, z = lax.axis_index("dom"), lax.axis_index("feat")
    core = lax.rem(d, 2)
    chip = d // 2
    x, y = lax.rem(chip, n), chip // n
    lane = lax.rem(d, LANES)
    base = d - lane
    wr = fl // LANES
    half = rows // HALVES
    piece = half // ORDERS
    greet(dom_count, nf)
    sends = []
    w_full[z, :, :hidden] = w_self[...]
    w_full[z, :, hidden:] = w_neigh[...]
    mine = rows_at(lane * wr, wr, wr)
    for i in range(1, nf):
        zt = lax.rem(z + i, nf)
        ref = w_full.at[z, mine, :]
        sends.append(send(ref, ref, w1s.at[i], w1r.at[z], {"feat": zt}))
    local = pltpu.make_async_copy(features.at[rows_at(z * rows, rows, rows), :], own.at[z], local_sem)
    local.start()
    for h in range(HALVES):
        for i in range(nf - 1, 0, -1):
            zt = lax.rem(z + i, nf)
            sends.append(send(
                features.at[rows_at(zt * rows + h * half, half, half), :],
                own.at[z, pl.ds(h * half, half), :],
                fs.at[h, i], fr.at[h, z], {"feat": zt},
            ))
    for i in range(1, dom_count):
        to = lax.rem(d + i, dom_count)
        sends.append(send(slots.at[to], table.at[d], ts.at[i], tr.at[d], {"dom": to}))
    table[d] = slots[d]
    for i in range(1, nf):
        zs = lax.rem(z + i, nf)
        ref = w_full.at[zs, mine, :]
        arrived(ref, w1r.at[zs])
        for j in range(1, LANES):
            to = base + lax.rem(lane + j, LANES)
            sends.append(send(ref, ref, w2s.at[i, j], w2r.at[zs, lane], {"dom": to}))
    for i in range(1, nf):
        zs = lax.rem(z + i, nf)
        for j in range(1, LANES):
            other = lax.rem(lane + j, LANES)
            arrived(w_full.at[zs, rows_at(other * wr, wr, wr), :], w2r.at[zs, other])
    local.wait()

    def place(order, first, second, which):
        if order == 0:
            return (second * n + first) * 2 + which
        return (first * n + second) * 2 + which

    for h in range(HALVES):
        span = pl.ds(h * half, half)
        for i in range(1, nf):
            zs = lax.rem(z + i, nf)
            arrived(own.at[zs, span, :], fr.at[h, zs])

        total = jnp.dot(own[0, span, :], w_full[0], preferred_element_type=F32)
        for k in range(1, nf):
            total += jnp.dot(own[k, span, :], w_full[k], preferred_element_type=F32)
        self_part[span, :] = total[:, :hidden]
        gathered[d, span, :] = total[:, hidden:].astype(BF16)

        def spread(block, c, sems, to):
            ref = gathered.at[block, pl.ds(c * piece, piece), :]
            sends.append(send(ref, ref, sems, agr.at[block, c], {"dom": to}))

        def came(block, c):
            arrived(gathered.at[block, pl.ds(c * piece, piece), :], agr.at[block, c])

        steps = []
        for o in range(ORDERS):
            c = h * ORDERS + o
            p1, p2 = (x, y) if o == 0 else (y, x)
            at = lambda i1, i2, which, o=o, p1=p1, p2=p2: place(
                o, lax.rem(p1 + i1, n), lax.rem(p2 + i2, n), which
            )
            steps.append((c, at))
        for c, at in steps:
            for i in range(1, n):
                spread(d, c, s1.at[c, i], at(i, 0, core))
            for i in range(1, n):
                spread(d, c, s2.at[c, 0, i], at(0, i, core))
            spread(d, c, s3.at[c, 0, 0], at(0, 0, 1 - core))
        for c, at in steps:
            for i1 in range(1, n):
                block = at(i1, 0, core)
                came(block, c)
                for i2 in range(1, n):
                    spread(block, c, s2.at[c, i1, i2], at(0, i2, core))
                spread(block, c, s3.at[c, i1, 0], at(0, 0, 1 - core))
        for c, at in steps:
            for i2 in range(1, n):
                for i1 in range(n):
                    block = at(i1, i2, core)
                    came(block, c)
                    spread(block, c, s3.at[c, i1, i2], at(0, 0, 1 - core))
    for c in range(HALVES * ORDERS):
        for b in range(dom_count // 2):
            block = b * 2 + 1 - core
            arrived(gathered.at[block, pl.ds(c * piece, piece), :], agr.at[block, c])
    for i in range(1, dom_count):
        other = lax.rem(d + i, dom_count)
        arrived(table.at[other], tr.at[other])
    for copy in sends:
        copy.wait_send()


def aggregate_kernel(
    sizes, local_refs, remote_refs, table, weights, self_part, out_grad, gathered,
    hidden_out, grad_self, partial, acc,
):
    dom_count, local_count, count, slot_count, tile, chips = sizes
    t = pl.program_id(0)
    d = lax.axis_index("dom")

    @pl.when(t == 0)
    def _():
        def clear(b, carry):
            acc[b] = jnp.zeros(acc.shape[1:], F32)
            return carry
        lax.fori_loop(0, dom_count, clear, 0)

    blocks, spans = [], []
    for k in range(count):
        if k < local_count:
            r, u = d, local_refs[t, k]
        else:
            q = remote_refs[t, k - local_count]
            r = q // slot_count
            u = table[r, q - r * slot_count]
        blocks.append(r)
        spans.append(rows_at(u * tile, tile, tile))
    degree = jnp.zeros((tile, tile), F32)
    summed = jnp.zeros((tile, gathered.shape[2]), F32)
    for k in range(0, count, 2):
        pair = range(k, min(k + 2, count))
        left = [weights[0, j] for j in pair]
        for w in left:
            degree += w.astype(F32)
        right = [gathered[blocks[j], spans[j], :] for j in pair]
        summed += jnp.dot(
            jnp.concatenate(left, axis=1), jnp.concatenate(right, axis=0),
            preferred_element_type=F32,
        )
    root = jnp.sqrt(jnp.sum(degree, axis=1, keepdims=True))
    preact = self_part[...] + summed / root
    logistic = jax.nn.sigmoid(preact)
    hidden_out[...] = (preact * logistic).astype(BF16)
    grad_pre = out_grad[...].astype(F32) * (logistic * (1.0 + preact * (1.0 - logistic)))
    grad_self[...] = grad_pre.astype(BF16)
    grad_agg = (grad_pre / root).astype(BF16)
    for k in range(count):
        contrib = lax.dot_general(
            weights[0, k], grad_agg, (((0,), (0,)), ((), ())), preferred_element_type=F32
        )
        at = lax.rem(blocks[k], 2) * chips + blocks[k] // 2
        acc[at, spans[k], :] += contrib

    @pl.when(t == pl.num_programs(0) - 1)
    def _():
        def finish(b, carry):
            partial[b] = acc[b].astype(BF16)
            return carry
        lax.fori_loop(0, dom_count, finish, 0)


def reduce_kernel(
    sizes, scale, partial, grad_self, own, w_full, grad_out, gw_self, gw_neigh,
    from_sib, sums, b1, b2, grad_proj, stage, gw, gw_recv, gw_sum, gw_cross, gw_z,
    local_sem, ss, sr, as1, ar1, as2, ar2, zs_, zr, g1s, g1r, gcs, gcr, g2s, g2r, g3s, g3r,
):
    dom_count, nf, rows, fl, hidden, n = sizes
    d, z = lax.axis_index("dom"), lax.axis_index("feat")
    core = lax.rem(d, 2)
    chip = d // 2
    x, y = lax.rem(chip, n), chip // n
    lane = lax.rem(d, LANES)
    base = d - lane
    wr = fl // LANES
    chunks = HALVES * ORDERS
    piece = rows // chunks
    groups = dom_count // LANES
    greet(dom_count, nf)
    sends, locals_ = [], []
    for c in range(chunks):
        span = pl.ds(c * piece, piece)
        sends.append(send(
            partial.at[1 - core, :, :, span, :], from_sib.at[:, :, span, :],
            ss.at[c], sr.at[c], {"dom": chip * 2 + 1 - core},
        ))
    grad_proj[:, :hidden] = grad_self[...]
    for c in range(chunks):
        span = pl.ds(c * piece, piece)
        arrived(from_sib.at[:, :, span, :], sr.at[c])
        for yy in range(n):
            for xx in range(n):
                sums[yy, xx, span, :] = (
                    partial[core, yy, xx, span, :].astype(F32)
                    + from_sib[yy, xx, span, :].astype(F32)
                ).astype(BF16)
        for i in range(1, n):
            if c % ORDERS == 0:
                xt = lax.rem(x + i, n)
                src, me, to = sums.at[:, xt, span, :], x, (y * n + xt) * 2 + core
            else:
                yt = lax.rem(y + i, n)
                src, me, to = sums.at[yt, :, span, :], y, (yt * n + x) * 2 + core
            sends.append(send(src, b1.at[me, :, span, :], as1.at[c, i], ar1.at[c, me], {"dom": to}))
    for c in range(chunks):
        span = pl.ds(c * piece, piece)
        me1, me2 = (x, y) if c % ORDERS == 0 else (y, x)
        for i in range(1, n):
            other = lax.rem(me1 + i, n)
            arrived(b1.at[other, :, span, :], ar1.at[c, other])
        for j in range(n):
            to2 = lax.rem(me2 + j, n)
            if c % ORDERS == 0:
                total = sums[to2, x, span, :].astype(F32)
            else:
                total = sums[y, to2, span, :].astype(F32)
            for i in range(1, n):
                total += b1[lax.rem(me1 + i, n), to2, span, :].astype(F32)
            b1[me1, to2, span, :] = total.astype(BF16)
            if j:
                to = ((to2 * n + x) if c % ORDERS == 0 else (y * n + to2)) * 2 + core
                sends.append(send(
                    b1.at[me1, to2, span, :], b2.at[me2, span, :], as2.at[c, j], ar2.at[c, me2],
                    {"dom": to},
                ))
    for c in range(chunks):
        span = pl.ds(c * piece, piece)
        me1, me2 = (x, y) if c % ORDERS == 0 else (y, x)
        total = b1[me1, me2, span, :].astype(F32)
        for i in range(1, n):
            other = lax.rem(me2 + i, n)
            arrived(b2.at[other, span, :], ar2.at[c, other])
            total += b2[other, span, :].astype(F32)
        grad_proj[span, hidden:] = total.astype(BF16)
        for i in range(nf - 1, -1, -1):
            zt = lax.rem(z + i, nf)
            stage[zt, span, :] = lax.dot_general(
                grad_proj[span, :], w_full[zt], (((1,), (1,)), ((), ())),
                preferred_element_type=F32,
            ).astype(BF16)
            target = grad_out.at[rows_at(z * rows + c * piece, piece, piece), :]
            if i:
                sends.append(send(
                    stage.at[zt, span, :], target, zs_.at[c, i], zr.at[c, z], {"feat": zt}
                ))
            else:
                copy = pltpu.make_async_copy(stage.at[zt, span, :], target, local_sem.at[c])
                copy.start()
                locals_.append(copy)
    for k in range(nf):
        gw[k] = lax.dot_general(
            own[k], grad_proj[...], (((0,), (0,)), ((), ())), preferred_element_type=F32
        ).astype(BF16)
    mine = rows_at(lane * wr, wr, wr)
    for j in range(1, LANES):
        other = lax.rem(lane + j, LANES)
        sends.append(send(
            gw.at[:, rows_at(other * wr, wr, wr), :], gw_recv.at[lane], g1s.at[j], g1r.at[lane],
            {"dom": base + other},
        ))
    total = gw[:, mine, :].astype(F32)
    for j in range(1, LANES):
        other = lax.rem(lane + j, LANES)
        arrived(gw_recv.at[other], g1r.at[other])
        total += gw_recv[other].astype(F32)
    gw_sum[...] = total
    if groups > 1:
        group = d // LANES
        gw_cross[group] = gw_sum[...]
        for j in range(1, groups):
            sends.append(send(
                gw_cross.at[group], gw_cross.at[group], gcs.at[j], gcr.at[group],
                {"dom": lax.rem(d + j * LANES, dom_count)},
            ))
        for j in range(1, groups):
            other = lax.rem(group + j, groups)
            arrived(gw_cross.at[other], gcr.at[other])
            total += gw_cross[other]
        gw_sum[...] = total
    for i in range(1, nf):
        zt = lax.rem(z + i, nf)
        sends.append(send(gw_sum.at[zt], gw_z.at[z], g2s.at[i], g2r.at[z], {"feat": zt}))
    final = gw_sum[z]
    for i in range(1, nf):
        zt = lax.rem(z + i, nf)
        arrived(gw_z.at[zt], g2r.at[zt])
        final += gw_z[zt]
    final = final * scale
    gw_self[mine, :] = final[:, :hidden]
    gw_neigh[mine, :] = final[:, hidden:]
    for j in range(1, LANES):
        to = {"dom": base + lax.rem(lane + j, LANES)}
        for which, ref in enumerate((gw_self, gw_neigh)):
            at = ref.at[mine, :]
            sends.append(send(at, at, g3s.at[which, j], g3r.at[which, lane], to))
    for j in range(1, LANES):
        other = lax.rem(lane + j, LANES)
        for which, ref in enumerate((gw_self, gw_neigh)):
            arrived(ref.at[rows_at(other * wr, wr, wr), :], g3r.at[which, other])
    for c in range(chunks):
        for i in range(1, nf):
            zt = lax.rem(z + i, nf)
            arrived(grad_out.at[rows_at(zt * rows + c * piece, piece, piece), :], zr.at[c, zt])
    for copy in locals_:
        copy.wait()
    for copy in sends:
        copy.wait_send()


def body(features, w_self, w_neigh, tile_weights, local_refs, remote_refs, send_tiles, out_grad):
    tile_count, count, tile = tile_weights.shape[:3]
    local_count = local_refs.shape[1]
    fl, hidden = w_self.shape
    rows = tile_count * tile
    dom_count, nf = lax.axis_size("dom"), lax.axis_size("feat")
    slot_count = send_tiles.shape[2]
    n = math.isqrt(dom_count // 2)
    chips = n * n
    chunks = HALVES * ORDERS
    node_total = rows * dom_count * nf
    vmem = pl.BlockSpec(memory_space=pltpu.VMEM)
    smem = pl.BlockSpec(memory_space=pltpu.SMEM)
    hbm = pl.BlockSpec(memory_space=pl.ANY)
    dma = pltpu.SemaphoreType.DMA
    sizes = (dom_count, nf, rows, fl, hidden, n)
    slots = jnp.zeros((dom_count, 8, 128), jnp.int32).at[:, 0, :slot_count].set(send_tiles[0])
    own, w_full, self_part, gathered, table = pl.pallas_call(
        functools.partial(project_kernel, sizes),
        out_shape=(
            jax.ShapeDtypeStruct((nf, rows, fl), BF16),
            jax.ShapeDtypeStruct((nf, fl, 2 * hidden), BF16),
            jax.ShapeDtypeStruct((rows, hidden), F32),
            jax.ShapeDtypeStruct((dom_count, rows, hidden), BF16),
            jax.ShapeDtypeStruct((dom_count, 8, 128), jnp.int32),
        ),
        in_specs=[hbm, vmem, vmem, vmem],
        out_specs=(vmem,) * 5,
        scratch_shapes=[
            dma, dma((nf,)), dma((nf,)), dma((nf, LANES)), dma((nf, LANES)),
            dma((HALVES, nf)), dma((HALVES, nf)), dma((dom_count,)), dma((dom_count,)),
            dma((chunks, n)), dma((chunks, n, n)), dma((chunks, n, n)), dma((dom_count, chunks)),
        ],
        compiler_params=pltpu.CompilerParams(
            collective_id=0, has_side_effects=True, vmem_limit_bytes=VMEM_LIMIT
        ),
    )(features, w_self, w_neigh, slots)

    hidden_out, grad_self, partial = pl.pallas_call(
        functools.partial(
            aggregate_kernel, (dom_count, local_count, count, slot_count, tile, chips)
        ),
        grid=(tile_count,),
        out_shape=(
            jax.ShapeDtypeStruct((rows, hidden), BF16),
            jax.ShapeDtypeStruct((rows, hidden), BF16),
            jax.ShapeDtypeStruct((dom_count, rows, hidden), BF16),
        ),
        in_specs=[
            smem, smem, smem,
            pl.BlockSpec((1, count, tile, tile), lambda t: (t, 0, 0, 0)),
            pl.BlockSpec((tile, hidden), lambda t: (t, 0)),
            pl.BlockSpec((tile, hidden), lambda t: (t, 0)),
            vmem,
        ],
        out_specs=(
            pl.BlockSpec((tile, hidden), lambda t: (t, 0)),
            pl.BlockSpec((tile, hidden), lambda t: (t, 0)),
            vmem,
        ),
        scratch_shapes=[pltpu.VMEM((dom_count, rows, hidden), F32)],
        compiler_params=pltpu.CompilerParams(vmem_limit_bytes=VMEM_LIMIT),
    )(local_refs, remote_refs, table[:, 0, :slot_count], tile_weights, self_part, out_grad, gathered)

    wr = fl // LANES
    groups = dom_count // LANES
    grad_out, gw_self, gw_neigh = pl.pallas_call(
        functools.partial(reduce_kernel, sizes, float(node_total) ** (-0.5)),
        out_shape=(
            jax.ShapeDtypeStruct((nf * rows, fl), BF16),
            jax.ShapeDtypeStruct((fl, hidden), F32),
            jax.ShapeDtypeStruct((fl, hidden), F32),
        ),
        in_specs=[vmem] * 4,
        out_specs=(hbm, vmem, vmem),
        scratch_shapes=[
            pltpu.VMEM((n, n, rows, hidden), BF16),
            pltpu.VMEM((n, n, rows, hidden), BF16),
            pltpu.VMEM((n, n, rows, hidden), BF16),
            pltpu.VMEM((n, rows, hidden), BF16),
            pltpu.VMEM((rows, 2 * hidden), BF16),
            pltpu.VMEM((nf, rows, fl), BF16),
            pltpu.VMEM((nf, fl, 2 * hidden), BF16),
            pltpu.VMEM((LANES, nf, wr, 2 * hidden), BF16),
            pltpu.VMEM((nf, wr, 2 * hidden), F32),
            pltpu.VMEM((groups, nf, wr, 2 * hidden), F32),
            pltpu.VMEM((nf, wr, 2 * hidden), F32),
            dma((chunks,)), dma((chunks,)), dma((chunks,)),
            dma((chunks, n)), dma((chunks, n)), dma((chunks, n)), dma((chunks, n)),
            dma((chunks, nf)), dma((chunks, nf)),
            dma((LANES,)), dma((LANES,)), dma((groups,)), dma((groups,)),
            dma((nf,)), dma((nf,)), dma((2, LANES)), dma((2, LANES)),
        ],
        compiler_params=pltpu.CompilerParams(
            collective_id=1, has_side_effects=True, vmem_limit_bytes=VMEM_LIMIT
        ),
    )(partial.reshape(2, n, n, rows, hidden), grad_self, own, w_full)
    return (hidden_out, grad_out, gw_self, gw_neigh)


def solution(mesh):
    placed = (
        P("dom", "feat"),
        P("feat", None),
        P("feat", None),
        P(("dom", "feat"), None, None, None),
        P(("dom", "feat"), None),
        P(("dom", "feat"), None),
        P(("dom", "feat"), None, None),
        P(("dom", "feat"), None),
    )
    return jax.shard_map(
        body,
        mesh=mesh,
        in_specs=placed,
        out_specs=(P(("dom", "feat"), None), P("dom", "feat"), P("feat", None), P("feat", None)),
        check_vma=False,
    )
```

```python
import functools
import math

import jax
import jax.numpy as jnp
from jax import lax
from jax.experimental import pallas as pl
from jax.experimental.pallas import tpu as pltpu
from jax.sharding import PartitionSpec as P

MESH = pl.DeviceIdType.MESH
F32 = jnp.float32
BF16 = jnp.bfloat16
LANES = 8
HALVES = 2
PIECES = 6
ORDERS = 2
MIB = 1024 * 1024


def send(src, dst, send_sem, recv_sem, where):
    copy = pltpu.make_async_remote_copy(
        src_ref=src, dst_ref=dst, send_sem=send_sem, recv_sem=recv_sem,
        device_id=where, device_id_type=MESH,
    )
    copy.start()
    return copy


def arrived(ref, sem):
    pltpu.make_async_remote_copy(
        src_ref=ref, dst_ref=ref, send_sem=sem, recv_sem=sem,
        device_id={"feat": lax.axis_index("feat")}, device_id_type=MESH,
    ).wait_recv()


def greet(dom_count, feat_count):
    d, z = lax.axis_index("dom"), lax.axis_index("feat")
    barrier = pltpu.get_barrier_semaphore()
    for i in range(1, dom_count):
        pl.semaphore_signal(
            barrier, inc=1, device_id={"dom": lax.rem(d + i, dom_count)}, device_id_type=MESH
        )
    for i in range(1, feat_count):
        pl.semaphore_signal(
            barrier, inc=1, device_id={"feat": lax.rem(z + i, feat_count)}, device_id_type=MESH
        )
    pl.semaphore_wait(barrier, dom_count + feat_count - 2)


def feat_order(z, nf):
    inner = (z + 1) // 2 % 2
    half = nf // 2
    far_first = [*range(half, nf), *range(1, half)]
    near_first = [*range(1, half), *range(nf - 1, half - 1, -1)]
    targets = []
    for far, near in zip(far_first, near_first):
        mask = inner * far + (1 - inner) * near
        target, bit = 0, 1
        while bit < nf:
            target = target + (z // bit + mask // bit) % 2 * bit
            bit *= 2
        targets.append(target)
    return targets


def rows_at(start, size, unit):
    return pl.ds(pl.multiple_of(start, unit), size)


def project_kernel(
    sizes, features, w_self, w_neigh, slots, own, w_full, self_part, gathered, table,
    local_sem, w1s, w1r, w2s, w2r, fs, fr, ts, tr, s1, s2, s3, agr,
):
    dom_count, nf, rows, fl, hidden, n = sizes
    d, z = lax.axis_index("dom"), lax.axis_index("feat")
    core = lax.rem(d, 2)
    chip = d // 2
    x, y = lax.rem(chip, n), chip // n
    lane = lax.rem(d, LANES)
    base = d - lane
    wr = fl // LANES
    half = rows // HALVES
    piece = half // ORDERS
    greet(dom_count, nf)
    sends = []
    w_full[z, :, :hidden] = w_self[...]
    w_full[z, :, hidden:] = w_neigh[...]
    mine = rows_at(lane * wr, wr, wr)
    for i in range(1, nf):
        zt = lax.rem(z + i, nf)
        ref = w_full.at[z, mine, :]
        sends.append(send(ref, ref, w1s.at[i], w1r.at[z], {"feat": zt}))
    local = pltpu.make_async_copy(features.at[rows_at(z * rows, rows, rows), :], own.at[z], local_sem)
    local.start()
    for h in range(HALVES):
        for i, zt in enumerate(feat_order(z, nf)):
            sends.append(send(
                features.at[rows_at(zt * rows + h * half, half, half), :],
                own.at[z, pl.ds(h * half, half), :],
                fs.at[h, i], fr.at[h, z], {"feat": zt},
            ))
    for i in range(1, dom_count):
        to = lax.rem(d + i, dom_count)
        sends.append(send(slots.at[0], table.at[d], ts.at[i], tr.at[d], {"dom": to}))
    table[d] = slots[0]
    for i in range(1, nf):
        zs = lax.rem(z + i, nf)
        ref = w_full.at[zs, mine, :]
        arrived(ref, w1r.at[zs])
        for j in range(1, LANES):
            to = base + lax.rem(lane + j, LANES)
            sends.append(send(ref, ref, w2s.at[i, j], w2r.at[zs, lane], {"dom": to}))
    for i in range(1, nf):
        zs = lax.rem(z + i, nf)
        for j in range(1, LANES):
            other = lax.rem(lane + j, LANES)
            arrived(w_full.at[zs, rows_at(other * wr, wr, wr), :], w2r.at[zs, other])
    local.wait()

    def place(order, first, second, which):
        if order == 0:
            return (second * n + first) * 2 + which
        return (first * n + second) * 2 + which

    for h in range(HALVES):
        span = pl.ds(h * half, half)
        for i in range(1, nf):
            zs = lax.rem(z + i, nf)
            arrived(own.at[zs, span, :], fr.at[h, zs])

        total = jnp.dot(own[0, span, :], w_full[0], preferred_element_type=F32)
        for k in range(1, nf):
            total += jnp.dot(own[k, span, :], w_full[k], preferred_element_type=F32)
        self_part[span, :] = total[:, :hidden]
        gathered[d, span, :] = total[:, hidden:].astype(BF16)

        def spread(block, c, sems, to):
            ref = gathered.at[block, pl.ds(c * piece, piece), :]
            sends.append(send(ref, ref, sems, agr.at[block, c], {"dom": to}))

        def came(block, c):
            arrived(gathered.at[block, pl.ds(c * piece, piece), :], agr.at[block, c])

        steps = []
        for o in range(ORDERS):
            c = h * ORDERS + o
            p1, p2 = (x, y) if o == 0 else (y, x)
            at = lambda i1, i2, which, o=o, p1=p1, p2=p2: place(
                o, lax.rem(p1 + i1, n), lax.rem(p2 + i2, n), which
            )
            steps.append((c, at))
        for c, at in steps:
            for i in range(1, n):
                spread(d, c, s1.at[c, i], at(i, 0, core))
            for i in range(1, n):
                spread(d, c, s2.at[c, 0, i], at(0, i, core))
            spread(d, c, s3.at[c, 0, 0], at(0, 0, 1 - core))
        for c, at in steps:
            for i1 in range(1, n):
                block = at(i1, 0, core)
                came(block, c)
                for i2 in range(1, n):
                    spread(block, c, s2.at[c, i1, i2], at(0, i2, core))
                spread(block, c, s3.at[c, i1, 0], at(0, 0, 1 - core))
        for c, at in steps:
            for i2 in range(1, n):
                for i1 in range(n):
                    block = at(i1, i2, core)
                    came(block, c)
                    spread(block, c, s3.at[c, i1, i2], at(0, 0, 1 - core))
    for c in range(HALVES * ORDERS):
        for b in range(dom_count // 2):
            block = b * 2 + 1 - core
            arrived(gathered.at[block, pl.ds(c * piece, piece), :], agr.at[block, c])
    for i in range(1, dom_count):
        other = lax.rem(d + i, dom_count)
        arrived(table.at[other], tr.at[other])
    for copy in sends:
        copy.wait_send()


def aggregate_kernel(
    sizes, local_refs, remote_refs, table, weights, self_part, out_grad, gathered,
    hidden_out, grad_self, partial, acc,
):
    dom_count, local_count, count, slot_count, tile, chips = sizes
    t = pl.program_id(0)
    d = lax.axis_index("dom")

    @pl.when(t == 0)
    def _():
        def clear(b, carry):
            acc[b] = jnp.zeros(acc.shape[1:], F32)
            return carry
        lax.fori_loop(0, dom_count, clear, 0)

    blocks, spans = [], []
    for k in range(count):
        if k < local_count:
            r, u = d, local_refs[t, k]
        else:
            q = remote_refs[t, k - local_count]
            r = q // slot_count
            u = table[r, d, q - r * slot_count]
        blocks.append(r)
        spans.append(rows_at(u * tile, tile, tile))
    degree = jnp.zeros((tile, tile), F32)
    summed = jnp.zeros((tile, gathered.shape[2]), F32)
    for k in range(0, count, 2):
        pair = range(k, min(k + 2, count))
        left = [weights[0, j] for j in pair]
        for w in left:
            degree += w.astype(F32)
        right = [gathered[blocks[j], spans[j], :] for j in pair]
        summed += jnp.dot(
            jnp.concatenate(left, axis=1), jnp.concatenate(right, axis=0),
            preferred_element_type=F32,
        )
    root = jnp.sqrt(jnp.sum(degree, axis=1, keepdims=True))
    preact = self_part[...] + summed / root
    logistic = jax.nn.sigmoid(preact)
    hidden_out[...] = (preact * logistic).astype(BF16)
    grad_pre = out_grad[...].astype(F32) * (logistic * (1.0 + preact * (1.0 - logistic)))
    grad_self[...] = grad_pre.astype(BF16)
    grad_agg = (grad_pre / root).astype(BF16)
    for k in range(count):
        contrib = lax.dot_general(
            weights[0, k], grad_agg, (((0,), (0,)), ((), ())), preferred_element_type=F32
        )
        at = lax.rem(blocks[k], 2) * chips + blocks[k] // 2
        acc[at, spans[k], :] += contrib

    @pl.when(t == pl.num_programs(0) - 1)
    def _():
        def finish(b, carry):
            partial[b] = acc[b].astype(BF16)
            return carry
        lax.fori_loop(0, dom_count, finish, 0)


def reduce_kernel(
    sizes, scale, partial, grad_self, own, w_full, grad_out, gw_self, gw_neigh,
    from_sib, sums, b1, b2, grad_proj, stage, gw, gw_recv, gw_sum, gw_cross, gw_z,
    ss, sr, as1, ar1, as2, ar2, zs_, zr, g1s, g1r, gcs, gcr, g2s, g2r, g3s, g3r,
):
    dom_count, nf, rows, fl, hidden, n = sizes
    d, z = lax.axis_index("dom"), lax.axis_index("feat")
    core = lax.rem(d, 2)
    chip = d // 2
    x, y = lax.rem(chip, n), chip // n
    lane = lax.rem(d, LANES)
    base = d - lane
    wr = fl // LANES
    chunks = PIECES
    piece = rows // chunks
    groups = dom_count // LANES
    greet(dom_count, nf)
    sends = []
    for c in range(chunks):
        span = pl.ds(c * piece, piece)
        sends.append(send(
            partial.at[1 - core, :, :, span, :], from_sib.at[:, :, span, :],
            ss.at[c], sr.at[c], {"dom": chip * 2 + 1 - core},
        ))
    grad_proj[:, :hidden] = grad_self[...]
    order = feat_order(z, nf)

    def combine(c):
        span = pl.ds(c * piece, piece)
        arrived(from_sib.at[:, :, span, :], sr.at[c])
        for yy in range(n):
            for xx in range(n):
                sums[yy, xx, span, :] = (
                    partial[core, yy, xx, span, :].astype(F32)
                    + from_sib[yy, xx, span, :].astype(F32)
                ).astype(BF16)
        for i in range(1, n):
            if c % ORDERS == 0:
                xt = lax.rem(x + i, n)
                src, me, to = sums.at[:, xt, span, :], x, (y * n + xt) * 2 + core
            else:
                yt = lax.rem(y + i, n)
                src, me, to = sums.at[yt, :, span, :], y, (yt * n + x) * 2 + core
            sends.append(send(src, b1.at[me, :, span, :], as1.at[c, i], ar1.at[c, me], {"dom": to}))

    def turn(c):
        span = pl.ds(c * piece, piece)
        me1, me2 = (x, y) if c % ORDERS == 0 else (y, x)
        for i in range(1, n):
            other = lax.rem(me1 + i, n)
            arrived(b1.at[other, :, span, :], ar1.at[c, other])
        for j in [*range(1, n), 0]:
            to2 = lax.rem(me2 + j, n)
            if c % ORDERS == 0:
                total = sums[to2, x, span, :].astype(F32)
            else:
                total = sums[y, to2, span, :].astype(F32)
            for i in range(1, n):
                total += b1[lax.rem(me1 + i, n), to2, span, :].astype(F32)
            b1[me1, to2, span, :] = total.astype(BF16)
            if j:
                to = ((to2 * n + x) if c % ORDERS == 0 else (y * n + to2)) * 2 + core
                sends.append(send(
                    b1.at[me1, to2, span, :], b2.at[me2, span, :], as2.at[c, j], ar2.at[c, me2],
                    {"dom": to},
                ))

    def settle(c):
        span = pl.ds(c * piece, piece)
        me1, me2 = (x, y) if c % ORDERS == 0 else (y, x)
        total = b1[me1, me2, span, :].astype(F32)
        for i in range(1, n):
            other = lax.rem(me2 + i, n)
            arrived(b2.at[other, span, :], ar2.at[c, other])
            total += b2[other, span, :].astype(F32)
        grad_proj[span, hidden:] = total.astype(BF16)

    def feature_rows(c, zt):
        span = pl.ds(c * piece, piece)
        return lax.dot_general(
            grad_proj[span, :], w_full[zt], (((1,), (1,)), ((), ())),
            preferred_element_type=F32,
        ).astype(BF16)

    def deliver(c):
        span = pl.ds(c * piece, piece)
        for i, zt in enumerate(order):
            stage[zt, span, :] = feature_rows(c, zt)
            sends.append(send(
                stage.at[zt, span, :],
                grad_out.at[rows_at(z * rows + c * piece, piece, piece), :],
                zs_.at[c, i], zr.at[c, z], {"feat": zt},
            ))

    def weigh(columns):
        for k in range(nf):
            gw[k, :, columns] = lax.dot_general(
                own[k], grad_proj[:, columns], (((0,), (0,)), ((), ())),
                preferred_element_type=F32,
            ).astype(BF16)

    plan = []
    for c in range(chunks + 2):
        if c < chunks:
            plan.append((combine, c))
        if 1 <= c <= chunks:
            plan.append((turn, c - 1))
        if c >= 2:
            plan.append((settle, c - 2))
            if c - 2 < chunks - 1:
                plan.append((deliver, c - 2))
        if c == 0:
            plan.append((weigh, slice(0, hidden)))
    for step, what in plan:
        step(what)
    weigh(slice(hidden, 2 * hidden))
    mine = rows_at(lane * wr, wr, wr)
    for j in range(1, LANES):
        other = lax.rem(lane + j, LANES)
        sends.append(send(
            gw.at[:, rows_at(other * wr, wr, wr), :], gw_recv.at[lane], g1s.at[j], g1r.at[lane],
            {"dom": base + other},
        ))
    total = gw[:, mine, :].astype(F32)
    for j in range(1, LANES):
        other = lax.rem(lane + j, LANES)
        arrived(gw_recv.at[other], g1r.at[other])
        total += gw_recv[other].astype(F32)
    gw_sum[...] = total
    if groups > 1:
        group = d // LANES
        gw_cross[group] = gw_sum[...]
        for j in range(1, groups):
            sends.append(send(
                gw_cross.at[group], gw_cross.at[group], gcs.at[j], gcr.at[group],
                {"dom": lax.rem(d + j * LANES, dom_count)},
            ))
        for j in range(1, groups):
            other = lax.rem(group + j, groups)
            arrived(gw_cross.at[other], gcr.at[other])
            total += gw_cross[other]
        gw_sum[...] = total
    for i in range(1, nf):
        zt = lax.rem(z + i, nf)
        sends.append(send(gw_sum.at[zt], gw_z.at[z], g2s.at[i], g2r.at[z], {"feat": zt}))
    deliver(chunks - 1)
    for c in range(chunks):
        grad_out[rows_at(z * rows + c * piece, piece, piece), :] = feature_rows(c, z)
    final = gw_sum[z]
    for i in range(1, nf):
        zt = lax.rem(z + i, nf)
        arrived(gw_z.at[zt], g2r.at[zt])
        final += gw_z[zt]
    final = final * scale
    gw_self[mine, :] = final[:, :hidden]
    gw_neigh[mine, :] = final[:, hidden:]
    for j in range(1, LANES):
        to = {"dom": base + lax.rem(lane + j, LANES)}
        for which, ref in enumerate((gw_self, gw_neigh)):
            at = ref.at[mine, :]
            sends.append(send(at, at, g3s.at[which, j], g3r.at[which, lane], to))
    for j in range(1, LANES):
        other = lax.rem(lane + j, LANES)
        for which, ref in enumerate((gw_self, gw_neigh)):
            arrived(ref.at[rows_at(other * wr, wr, wr), :], g3r.at[which, other])
    for c in range(chunks):
        for i in range(1, nf):
            zt = lax.rem(z + i, nf)
            arrived(grad_out.at[rows_at(zt * rows + c * piece, piece, piece), :], zr.at[c, zt])
    for copy in sends:
        copy.wait_send()


def body(features, w_self, w_neigh, tile_weights, local_refs, remote_refs, send_tiles, out_grad):
    tile_count, count, tile = tile_weights.shape[:3]
    local_count = local_refs.shape[1]
    fl, hidden = w_self.shape
    rows = tile_count * tile
    dom_count, nf = lax.axis_size("dom"), lax.axis_size("feat")
    slot_count = send_tiles.shape[2]
    n = math.isqrt(dom_count // 2)
    chips = n * n
    chunks = HALVES * ORDERS
    node_total = rows * dom_count * nf
    vmem_limit = min(60, 8 + 2 * dom_count) * MIB
    vmem = pl.BlockSpec(memory_space=pltpu.VMEM)
    smem = pl.BlockSpec(memory_space=pltpu.SMEM)
    hbm = pl.BlockSpec(memory_space=pl.ANY)
    dma = pltpu.SemaphoreType.DMA
    sizes = (dom_count, nf, rows, fl, hidden, n)
    own, w_full, self_part, gathered, table = pl.pallas_call(
        functools.partial(project_kernel, sizes),
        out_shape=(
            jax.ShapeDtypeStruct((nf, rows, fl), BF16),
            jax.ShapeDtypeStruct((nf, fl, 2 * hidden), BF16),
            jax.ShapeDtypeStruct((rows, hidden), F32),
            jax.ShapeDtypeStruct((dom_count, rows, hidden), BF16),
            jax.ShapeDtypeStruct((dom_count, dom_count, slot_count), jnp.int32),
        ),
        in_specs=[hbm, vmem, vmem, vmem],
        out_specs=(vmem,) * 5,
        scratch_shapes=[
            dma, dma((nf,)), dma((nf,)), dma((nf, LANES)), dma((nf, LANES)),
            dma((HALVES, nf)), dma((HALVES, nf)), dma((dom_count,)), dma((dom_count,)),
            dma((chunks, n)), dma((chunks, n, n)), dma((chunks, n, n)), dma((dom_count, chunks)),
        ],
        compiler_params=pltpu.CompilerParams(
            collective_id=0, has_side_effects=True, vmem_limit_bytes=vmem_limit
        ),
    )(features, w_self, w_neigh, send_tiles)

    hidden_out, grad_self, partial = pl.pallas_call(
        functools.partial(
            aggregate_kernel, (dom_count, local_count, count, slot_count, tile, chips)
        ),
        grid=(tile_count,),
        out_shape=(
            jax.ShapeDtypeStruct((rows, hidden), BF16),
            jax.ShapeDtypeStruct((rows, hidden), BF16),
            jax.ShapeDtypeStruct((dom_count, rows, hidden), BF16),
        ),
        in_specs=[
            smem, smem, smem,
            pl.BlockSpec((1, count, tile, tile), lambda t: (t, 0, 0, 0)),
            pl.BlockSpec((tile, hidden), lambda t: (t, 0)),
            pl.BlockSpec((tile, hidden), lambda t: (t, 0)),
            vmem,
        ],
        out_specs=(
            pl.BlockSpec((tile, hidden), lambda t: (t, 0)),
            pl.BlockSpec((tile, hidden), lambda t: (t, 0)),
            vmem,
        ),
        scratch_shapes=[pltpu.VMEM((dom_count, rows, hidden), F32)],
        compiler_params=pltpu.CompilerParams(vmem_limit_bytes=vmem_limit),
    )(local_refs, remote_refs, table, tile_weights, self_part, out_grad, gathered)

    wr = fl // LANES
    groups = dom_count // LANES
    grad_out, gw_self, gw_neigh = pl.pallas_call(
        functools.partial(reduce_kernel, sizes, float(node_total) ** (-0.5)),
        out_shape=(
            jax.ShapeDtypeStruct((nf * rows, fl), BF16),
            jax.ShapeDtypeStruct((fl, hidden), F32),
            jax.ShapeDtypeStruct((fl, hidden), F32),
        ),
        in_specs=[vmem] * 4,
        out_specs=(vmem,) * 3,
        scratch_shapes=[
            pltpu.VMEM((n, n, rows, hidden), BF16),
            pltpu.VMEM((n, n, rows, hidden), BF16),
            pltpu.VMEM((n, n, rows, hidden), BF16),
            pltpu.VMEM((n, rows, hidden), BF16),
            pltpu.VMEM((rows, 2 * hidden), BF16),
            pltpu.VMEM((nf, rows, fl), BF16),
            pltpu.VMEM((nf, fl, 2 * hidden), BF16),
            pltpu.VMEM((LANES, nf, wr, 2 * hidden), BF16),
            pltpu.VMEM((nf, wr, 2 * hidden), F32),
            pltpu.VMEM((groups, nf, wr, 2 * hidden), F32),
            pltpu.VMEM((nf, wr, 2 * hidden), F32),
            dma((PIECES,)), dma((PIECES,)),
            dma((PIECES, n)), dma((PIECES, n)), dma((PIECES, n)), dma((PIECES, n)),
            dma((PIECES, nf)), dma((PIECES, nf)),
            dma((LANES,)), dma((LANES,)), dma((groups,)), dma((groups,)),
            dma((nf,)), dma((nf,)), dma((2, LANES)), dma((2, LANES)),
        ],
        compiler_params=pltpu.CompilerParams(
            collective_id=1, has_side_effects=True, vmem_limit_bytes=vmem_limit
        ),
    )(partial.reshape(2, n, n, rows, hidden), grad_self, own, w_full)
    return (hidden_out, grad_out, gw_self, gw_neigh)


def solution(mesh):
    placed = (
        P("dom", "feat"),
        P("feat", None),
        P("feat", None),
        P(("dom", "feat"), None, None, None),
        P(("dom", "feat"), None),
        P(("dom", "feat"), None),
        P(("dom", "feat"), None, None),
        P(("dom", "feat"), None),
    )
    return jax.shard_map(
        body,
        mesh=mesh,
        in_specs=placed,
        out_specs=(P(("dom", "feat"), None), P("dom", "feat"), P("feat", None), P("feat", None)),
        check_vma=False,
    )
```

```python
import functools
import math

import jax
import jax.numpy as jnp
from jax import lax
from jax.experimental import pallas as pl
from jax.experimental.pallas import tpu as pltpu
from jax.sharding import PartitionSpec as P

MESH = pl.DeviceIdType.MESH
F32 = jnp.float32
BF16 = jnp.bfloat16
LANES = 8
HALVES = 2
PIECES = 6
ORDERS = 2
MIB = 1024 * 1024


def send(src, dst, send_sem, recv_sem, where):
    copy = pltpu.make_async_remote_copy(
        src_ref=src, dst_ref=dst, send_sem=send_sem, recv_sem=recv_sem,
        device_id=where, device_id_type=MESH,
    )
    copy.start()
    return copy


def arrived(ref, sem):
    pltpu.make_async_remote_copy(
        src_ref=ref, dst_ref=ref, send_sem=sem, recv_sem=sem,
        device_id={"feat": lax.axis_index("feat")}, device_id_type=MESH,
    ).wait_recv()


def greet(dom_count, feat_count):
    d, z = lax.axis_index("dom"), lax.axis_index("feat")
    barrier = pltpu.get_barrier_semaphore()
    for i in range(1, dom_count):
        pl.semaphore_signal(
            barrier, inc=1, device_id={"dom": lax.rem(d + i, dom_count)}, device_id_type=MESH
        )
    for i in range(1, feat_count):
        pl.semaphore_signal(
            barrier, inc=1, device_id={"feat": lax.rem(z + i, feat_count)}, device_id_type=MESH
        )
    pl.semaphore_wait(barrier, dom_count + feat_count - 2)


def feat_order(z, nf):
    inner = (z + 1) // 2 % 2
    half = nf // 2
    far_first = [*range(half, nf), *range(1, half)]
    near_first = [*range(1, half), *range(nf - 1, half - 1, -1)]
    targets = []
    for far, near in zip(far_first, near_first):
        mask = inner * far + (1 - inner) * near
        target, bit = 0, 1
        while bit < nf:
            target = target + (z // bit + mask // bit) % 2 * bit
            bit *= 2
        targets.append(target)
    return targets


def rows_at(start, size, unit):
    return pl.ds(pl.multiple_of(start, unit), size)


def project_kernel(
    sizes, features, w_self, w_neigh, slots, own, w_full, self_part, gathered, table,
    local_sem, w1s, w1r, w2s, w2r, fs, fr, ts, tr, s1, s2, s3, agr,
):
    dom_count, nf, rows, fl, hidden, n = sizes
    d, z = lax.axis_index("dom"), lax.axis_index("feat")
    core = lax.rem(d, 2)
    chip = d // 2
    x, y = lax.rem(chip, n), chip // n
    lane = lax.rem(d, LANES)
    base = d - lane
    wr = fl // LANES
    half = rows // HALVES
    piece = half // ORDERS
    greet(dom_count, nf)
    sends = []
    w_full[z, :, :hidden] = w_self[...]
    w_full[z, :, hidden:] = w_neigh[...]
    mine = rows_at(lane * wr, wr, wr)
    for i in range(1, nf):
        zt = lax.rem(z + i, nf)
        ref = w_full.at[z, mine, :]
        sends.append(send(ref, ref, w1s.at[i], w1r.at[z], {"feat": zt}))
    local = pltpu.make_async_copy(features.at[rows_at(z * rows, rows, rows), :], own.at[z], local_sem)
    local.start()
    for h in range(HALVES):
        for i, zt in enumerate(feat_order(z, nf)):
            sends.append(send(
                features.at[rows_at(zt * rows + h * half, half, half), :],
                own.at[z, pl.ds(h * half, half), :],
                fs.at[h, i], fr.at[h, z], {"feat": zt},
            ))
    for i in range(1, dom_count):
        to = lax.rem(d + i, dom_count)
        sends.append(send(slots.at[0], table.at[d], ts.at[i], tr.at[d], {"dom": to}))
    table[d] = slots[0]
    for i in range(1, nf):
        zs = lax.rem(z + i, nf)
        ref = w_full.at[zs, mine, :]
        arrived(ref, w1r.at[zs])
        for j in range(1, LANES):
            to = base + lax.rem(lane + j, LANES)
            sends.append(send(ref, ref, w2s.at[i, j], w2r.at[zs, lane], {"dom": to}))
    for i in range(1, nf):
        zs = lax.rem(z + i, nf)
        for j in range(1, LANES):
            other = lax.rem(lane + j, LANES)
            arrived(w_full.at[zs, rows_at(other * wr, wr, wr), :], w2r.at[zs, other])
    local.wait()

    def place(order, first, second, which):
        if order == 0:
            return (second * n + first) * 2 + which
        return (first * n + second) * 2 + which

    for h in range(HALVES):
        span = pl.ds(h * half, half)
        for i in range(1, nf):
            zs = lax.rem(z + i, nf)
            arrived(own.at[zs, span, :], fr.at[h, zs])

        total = jnp.dot(own[0, span, :], w_full[0], preferred_element_type=F32)
        for k in range(1, nf):
            total += jnp.dot(own[k, span, :], w_full[k], preferred_element_type=F32)
        self_part[span, :] = total[:, :hidden]
        gathered[d, span, :] = total[:, hidden:].astype(BF16)

        def spread(block, c, sems, to):
            ref = gathered.at[block, pl.ds(c * piece, piece), :]
            sends.append(send(ref, ref, sems, agr.at[block, c], {"dom": to}))

        def came(block, c):
            arrived(gathered.at[block, pl.ds(c * piece, piece), :], agr.at[block, c])

        steps = []
        for o in range(ORDERS):
            c = h * ORDERS + o
            p1, p2 = (x, y) if o == 0 else (y, x)
            at = lambda i1, i2, which, o=o, p1=p1, p2=p2: place(
                o, lax.rem(p1 + i1, n), lax.rem(p2 + i2, n), which
            )
            steps.append((c, at))
        for c, at in steps:
            for i in range(1, n):
                spread(d, c, s1.at[c, i], at(i, 0, core))
            for i in range(1, n):
                spread(d, c, s2.at[c, 0, i], at(0, i, core))
            spread(d, c, s3.at[c, 0, 0], at(0, 0, 1 - core))
        for c, at in steps:
            for i1 in range(1, n):
                block = at(i1, 0, core)
                came(block, c)
                for i2 in range(1, n):
                    spread(block, c, s2.at[c, i1, i2], at(0, i2, core))
                spread(block, c, s3.at[c, i1, 0], at(0, 0, 1 - core))
        for c, at in steps:
            for i2 in range(1, n):
                for i1 in range(n):
                    block = at(i1, i2, core)
                    came(block, c)
                    spread(block, c, s3.at[c, i1, i2], at(0, 0, 1 - core))
    for c in range(HALVES * ORDERS):
        for b in range(dom_count // 2):
            block = b * 2 + 1 - core
            arrived(gathered.at[block, pl.ds(c * piece, piece), :], agr.at[block, c])
    for i in range(1, dom_count):
        other = lax.rem(d + i, dom_count)
        arrived(table.at[other], tr.at[other])
    for copy in sends:
        copy.wait_send()


def aggregate_kernel(
    sizes, local_refs, remote_refs, table, weights, self_part, out_grad, gathered,
    hidden_out, grad_self, partial, acc,
):
    dom_count, local_count, count, slot_count, tile, chips = sizes
    t = pl.program_id(0)
    d = lax.axis_index("dom")

    @pl.when(t == 0)
    def _():
        def clear(b, carry):
            acc[b] = jnp.zeros(acc.shape[1:], F32)
            return carry
        lax.fori_loop(0, dom_count, clear, 0)

    blocks, spans = [], []
    for k in range(count):
        if k < local_count:
            r, u = d, local_refs[t, k]
        else:
            q = remote_refs[t, k - local_count]
            r = q // slot_count
            u = table[r, d, q - r * slot_count]
        blocks.append(r)
        spans.append(rows_at(u * tile, tile, tile))
    degree = jnp.zeros((tile, tile), F32)
    summed = jnp.zeros((tile, gathered.shape[2]), F32)
    for k in range(0, count, 2):
        pair = range(k, min(k + 2, count))
        left = [weights[0, j] for j in pair]
        for w in left:
            degree += w.astype(F32)
        right = [gathered[blocks[j], spans[j], :] for j in pair]
        summed += jnp.dot(
            jnp.concatenate(left, axis=1), jnp.concatenate(right, axis=0),
            preferred_element_type=F32,
        )
    root = jnp.sqrt(jnp.sum(degree, axis=1, keepdims=True))
    preact = self_part[...] + summed / root
    logistic = jax.nn.sigmoid(preact)
    hidden_out[...] = (preact * logistic).astype(BF16)
    grad_pre = out_grad[...].astype(F32) * (logistic * (1.0 + preact * (1.0 - logistic)))
    grad_self[...] = grad_pre.astype(BF16)
    grad_agg = (grad_pre / root).astype(BF16)
    for k in range(count):
        contrib = lax.dot_general(
            weights[0, k], grad_agg, (((0,), (0,)), ((), ())), preferred_element_type=F32
        )
        at = lax.rem(blocks[k], 2) * chips + blocks[k] // 2
        acc[at, spans[k], :] += contrib

    @pl.when(t == pl.num_programs(0) - 1)
    def _():
        def finish(b, carry):
            partial[b] = acc[b].astype(BF16)
            return carry
        lax.fori_loop(0, dom_count, finish, 0)


def reduce_kernel(
    sizes, scale, partial, grad_self, own, w_full, grad_out, gw_self, gw_neigh,
    from_sib, sums, b1, b2, grad_proj, stage, gw, gw_recv, gw_sum, gw_cross, gw_z,
    ss, sr, as1, ar1, as2, ar2, zs_, zr, g1s, g1r, gcs, gcr, g2s, g2r, g3s, g3r,
):
    dom_count, nf, rows, fl, hidden, n = sizes
    d, z = lax.axis_index("dom"), lax.axis_index("feat")
    core = lax.rem(d, 2)
    chip = d // 2
    x, y = lax.rem(chip, n), chip // n
    lane = lax.rem(d, LANES)
    base = d - lane
    wr = fl // LANES
    chunks = PIECES
    piece = rows // chunks
    groups = dom_count // LANES
    greet(dom_count, nf)
    sends = []
    for c in range(chunks):
        span = pl.ds(c * piece, piece)
        sends.append(send(
            partial.at[1 - core, :, :, span, :], from_sib.at[:, :, span, :],
            ss.at[c], sr.at[c], {"dom": chip * 2 + 1 - core},
        ))
    grad_proj[:, :hidden] = grad_self[...]
    order = feat_order(z, nf)

    def combine(c):
        span = pl.ds(c * piece, piece)
        arrived(from_sib.at[:, :, span, :], sr.at[c])
        for yy in range(n):
            for xx in range(n):
                sums[yy, xx, span, :] = (
                    partial[core, yy, xx, span, :].astype(F32)
                    + from_sib[yy, xx, span, :].astype(F32)
                ).astype(BF16)
        for i in range(1, n):
            if c % ORDERS == 0:
                xt = lax.rem(x + i, n)
                src, me, to = sums.at[:, xt, span, :], x, (y * n + xt) * 2 + core
            else:
                yt = lax.rem(y + i, n)
                src, me, to = sums.at[yt, :, span, :], y, (yt * n + x) * 2 + core
            sends.append(send(src, b1.at[me, :, span, :], as1.at[c, i], ar1.at[c, me], {"dom": to}))

    def turn(c):
        span = pl.ds(c * piece, piece)
        me1, me2 = (x, y) if c % ORDERS == 0 else (y, x)
        for i in range(1, n):
            other = lax.rem(me1 + i, n)
            arrived(b1.at[other, :, span, :], ar1.at[c, other])
        for j in [*range(1, n), 0]:
            to2 = lax.rem(me2 + j, n)
            if c % ORDERS == 0:
                total = sums[to2, x, span, :].astype(F32)
            else:
                total = sums[y, to2, span, :].astype(F32)
            for i in range(1, n):
                total += b1[lax.rem(me1 + i, n), to2, span, :].astype(F32)
            b1[me1, to2, span, :] = total.astype(BF16)
            if j:
                to = ((to2 * n + x) if c % ORDERS == 0 else (y * n + to2)) * 2 + core
                sends.append(send(
                    b1.at[me1, to2, span, :], b2.at[me2, span, :], as2.at[c, j], ar2.at[c, me2],
                    {"dom": to},
                ))

    def settle(c):
        span = pl.ds(c * piece, piece)
        me1, me2 = (x, y) if c % ORDERS == 0 else (y, x)
        total = b1[me1, me2, span, :].astype(F32)
        for i in range(1, n):
            other = lax.rem(me2 + i, n)
            arrived(b2.at[other, span, :], ar2.at[c, other])
            total += b2[other, span, :].astype(F32)
        grad_proj[span, hidden:] = total.astype(BF16)

    def feature_rows(c, zt):
        span = pl.ds(c * piece, piece)
        return lax.dot_general(
            grad_proj[span, :], w_full[zt], (((1,), (1,)), ((), ())),
            preferred_element_type=F32,
        ).astype(BF16)

    def deliver(c):
        span = pl.ds(c * piece, piece)
        for i, zt in enumerate(order):
            stage[zt, span, :] = feature_rows(c, zt)
            sends.append(send(
                stage.at[zt, span, :],
                grad_out.at[rows_at(z * rows + c * piece, piece, piece), :],
                zs_.at[c, i], zr.at[c, z], {"feat": zt},
            ))

    def weigh(columns):
        for k in range(nf):
            gw[k, :, columns] = lax.dot_general(
                own[k], grad_proj[:, columns], (((0,), (0,)), ((), ())),
                preferred_element_type=F32,
            ).astype(BF16)

    plan = []
    for c in range(chunks + 2):
        if c < chunks:
            plan.append((combine, c))
        if 1 <= c <= chunks:
            plan.append((turn, c - 1))
        if c >= 2:
            plan.append((settle, c - 2))
            if c - 2 < chunks - 2:
                plan.append((deliver, c - 2))
        if c == 0:
            plan.append((weigh, slice(0, hidden)))
    for step, what in plan:
        step(what)
    weigh(slice(hidden, 2 * hidden))
    mine = rows_at(lane * wr, wr, wr)
    for j in range(1, LANES):
        other = lax.rem(lane + j, LANES)
        sends.append(send(
            gw.at[:, rows_at(other * wr, wr, wr), :], gw_recv.at[lane], g1s.at[j], g1r.at[lane],
            {"dom": base + other},
        ))
    total = gw[:, mine, :].astype(F32)
    for j in range(1, LANES):
        other = lax.rem(lane + j, LANES)
        arrived(gw_recv.at[other], g1r.at[other])
        total += gw_recv[other].astype(F32)
    gw_sum[...] = total
    if groups > 1:
        group = d // LANES
        gw_cross[group] = gw_sum[...]
        for j in range(1, groups):
            sends.append(send(
                gw_cross.at[group], gw_cross.at[group], gcs.at[j], gcr.at[group],
                {"dom": lax.rem(d + j * LANES, dom_count)},
            ))
        for j in range(1, groups):
            other = lax.rem(group + j, groups)
            arrived(gw_cross.at[other], gcr.at[other])
            total += gw_cross[other]
        gw_sum[...] = total
    for i in range(1, nf):
        zt = lax.rem(z + i, nf)
        sends.append(send(gw_sum.at[zt], gw_z.at[z], g2s.at[i], g2r.at[z], {"feat": zt}))
    deliver(chunks - 2)
    deliver(chunks - 1)
    for c in range(chunks):
        grad_out[rows_at(z * rows + c * piece, piece, piece), :] = feature_rows(c, z)
    final = gw_sum[z]
    for i in range(1, nf):
        zt = lax.rem(z + i, nf)
        arrived(gw_z.at[zt], g2r.at[zt])
        final += gw_z[zt]
    final = final * scale
    gw_self[mine, :] = final[:, :hidden]
    gw_neigh[mine, :] = final[:, hidden:]
    for j in range(1, LANES):
        to = {"dom": base + lax.rem(lane + j, LANES)}
        for which, ref in enumerate((gw_self, gw_neigh)):
            at = ref.at[mine, :]
            sends.append(send(at, at, g3s.at[which, j], g3r.at[which, lane], to))
    for j in range(1, LANES):
        other = lax.rem(lane + j, LANES)
        for which, ref in enumerate((gw_self, gw_neigh)):
            arrived(ref.at[rows_at(other * wr, wr, wr), :], g3r.at[which, other])
    for c in range(chunks):
        for i in range(1, nf):
            zt = lax.rem(z + i, nf)
            arrived(grad_out.at[rows_at(zt * rows + c * piece, piece, piece), :], zr.at[c, zt])
    for copy in sends:
        copy.wait_send()


def body(features, w_self, w_neigh, tile_weights, local_refs, remote_refs, send_tiles, out_grad):
    tile_count, count, tile = tile_weights.shape[:3]
    local_count = local_refs.shape[1]
    fl, hidden = w_self.shape
    rows = tile_count * tile
    dom_count, nf = lax.axis_size("dom"), lax.axis_size("feat")
    slot_count = send_tiles.shape[2]
    n = math.isqrt(dom_count // 2)
    chips = n * n
    chunks = HALVES * ORDERS
    node_total = rows * dom_count * nf
    vmem_limit = min(60, 8 + 2 * dom_count) * MIB
    vmem = pl.BlockSpec(memory_space=pltpu.VMEM)
    smem = pl.BlockSpec(memory_space=pltpu.SMEM)
    hbm = pl.BlockSpec(memory_space=pl.ANY)
    dma = pltpu.SemaphoreType.DMA
    sizes = (dom_count, nf, rows, fl, hidden, n)
    own, w_full, self_part, gathered, table = pl.pallas_call(
        functools.partial(project_kernel, sizes),
        out_shape=(
            jax.ShapeDtypeStruct((nf, rows, fl), BF16),
            jax.ShapeDtypeStruct((nf, fl, 2 * hidden), BF16),
            jax.ShapeDtypeStruct((rows, hidden), F32),
            jax.ShapeDtypeStruct((dom_count, rows, hidden), BF16),
            jax.ShapeDtypeStruct((dom_count, dom_count, slot_count), jnp.int32),
        ),
        in_specs=[hbm, vmem, vmem, vmem],
        out_specs=(vmem,) * 5,
        scratch_shapes=[
            dma, dma((nf,)), dma((nf,)), dma((nf, LANES)), dma((nf, LANES)),
            dma((HALVES, nf)), dma((HALVES, nf)), dma((dom_count,)), dma((dom_count,)),
            dma((chunks, n)), dma((chunks, n, n)), dma((chunks, n, n)), dma((dom_count, chunks)),
        ],
        compiler_params=pltpu.CompilerParams(
            collective_id=0, has_side_effects=True, vmem_limit_bytes=vmem_limit
        ),
    )(features, w_self, w_neigh, send_tiles)

    hidden_out, grad_self, partial = pl.pallas_call(
        functools.partial(
            aggregate_kernel, (dom_count, local_count, count, slot_count, tile, chips)
        ),
        grid=(tile_count,),
        out_shape=(
            jax.ShapeDtypeStruct((rows, hidden), BF16),
            jax.ShapeDtypeStruct((rows, hidden), BF16),
            jax.ShapeDtypeStruct((dom_count, rows, hidden), BF16),
        ),
        in_specs=[
            smem, smem, smem,
            pl.BlockSpec((1, count, tile, tile), lambda t: (t, 0, 0, 0)),
            pl.BlockSpec((tile, hidden), lambda t: (t, 0)),
            pl.BlockSpec((tile, hidden), lambda t: (t, 0)),
            vmem,
        ],
        out_specs=(
            pl.BlockSpec((tile, hidden), lambda t: (t, 0)),
            pl.BlockSpec((tile, hidden), lambda t: (t, 0)),
            vmem,
        ),
        scratch_shapes=[pltpu.VMEM((dom_count, rows, hidden), F32)],
        compiler_params=pltpu.CompilerParams(vmem_limit_bytes=vmem_limit),
    )(local_refs, remote_refs, table, tile_weights, self_part, out_grad, gathered)

    wr = fl // LANES
    groups = dom_count // LANES
    grad_out, gw_self, gw_neigh = pl.pallas_call(
        functools.partial(reduce_kernel, sizes, float(node_total) ** (-0.5)),
        out_shape=(
            jax.ShapeDtypeStruct((nf * rows, fl), BF16),
            jax.ShapeDtypeStruct((fl, hidden), F32),
            jax.ShapeDtypeStruct((fl, hidden), F32),
        ),
        in_specs=[vmem] * 4,
        out_specs=(vmem,) * 3,
        scratch_shapes=[
            pltpu.VMEM((n, n, rows, hidden), BF16),
            pltpu.VMEM((n, n, rows, hidden), BF16),
            pltpu.VMEM((n, n, rows, hidden), BF16),
            pltpu.VMEM((n, rows, hidden), BF16),
            pltpu.VMEM((rows, 2 * hidden), BF16),
            pltpu.VMEM((nf, rows, fl), BF16),
            pltpu.VMEM((nf, fl, 2 * hidden), BF16),
            pltpu.VMEM((LANES, nf, wr, 2 * hidden), BF16),
            pltpu.VMEM((nf, wr, 2 * hidden), F32),
            pltpu.VMEM((groups, nf, wr, 2 * hidden), F32),
            pltpu.VMEM((nf, wr, 2 * hidden), F32),
            dma((PIECES,)), dma((PIECES,)),
            dma((PIECES, n)), dma((PIECES, n)), dma((PIECES, n)), dma((PIECES, n)),
            dma((PIECES, nf)), dma((PIECES, nf)),
            dma((LANES,)), dma((LANES,)), dma((groups,)), dma((groups,)),
            dma((nf,)), dma((nf,)), dma((2, LANES)), dma((2, LANES)),
        ],
        compiler_params=pltpu.CompilerParams(
            collective_id=1, has_side_effects=True, vmem_limit_bytes=vmem_limit
        ),
    )(partial.reshape(2, n, n, rows, hidden), grad_self, own, w_full)
    return (hidden_out, grad_out, gw_self, gw_neigh)


def solution(mesh):
    placed = (
        P("dom", "feat"),
        P("feat", None),
        P("feat", None),
        P(("dom", "feat"), None, None, None),
        P(("dom", "feat"), None),
        P(("dom", "feat"), None),
        P(("dom", "feat"), None, None),
        P(("dom", "feat"), None),
    )
    return jax.shard_map(
        body,
        mesh=mesh,
        in_specs=placed,
        out_specs=(P(("dom", "feat"), None), P("dom", "feat"), P("feat", None), P("feat", None)),
        check_vma=False,
    )
```
